128 devices in a mesh: dp: 32 (over y, x_hi, z), section: 4 (over x_lo, core).
Axes of the slice: x: 4 (x_hi: 2, x_lo: 2; x = x_hi * 2 + x_lo), y: 4, z: 4, core: 2. Of those that a mesh axis runs over, the one named last changes fastest.
Arguments:
- section_inputs: bfloat16 [4, 12288, 3072], P('section', 'dp'), may hold values from -6 to 6
- weights: bfloat16 [4, 3072, 3072], P('section'), may hold values from -0.109375 to 0.109375
- output_grads: bfloat16 [4, 12288, 3072], P('section', 'dp'), may hold values from -3 to 3
- warm_start: bfloat16 [4, 8, 3072], P('section'), may hold values from -0.109375 to 0.109375
Outputs:
- arrived: bfloat16 [4, 12288, 3072], P('section', 'dp')
- left_factor: float32 [4, 8, 3072], P('section')
- right_factor: float32 [4, 8, 3072], P('section')
The draws below stay inside these ranges and needn't reach their ends.
All inputs are finite; a program needn't handle non-finite values.
Results may differ from the reference program's by a relative error of at most 0.0085.
Values may be sent and summed in bfloat16 or wider, within the bound.
No kernel may reach another device: no remote copies, remote signals or barrier semaphores. Data moves between devices by JAX's collectives and lax.ppermute only.
A program may use at most 128 MiB of HBM per device.

```python
import jax
import jax.numpy as jnp
from jax import lax

D_IN = 3072
D_OUT = 3072
RANK = 8
ALL_ROWS = 12288
N_DP = 32
N_SECTION = 4


def block_scale(rng, extent, shards, low, top_value):
    gain = 1.0
    for dim, blocks in shards:
        heights = jax.random.uniform(jax.random.fold_in(jax.random.fold_in(rng, 6), dim), (blocks,), jnp.float32, low / len(shards), top_value / len(shards))
        gain = gain * jnp.repeat(jnp.exp(heights), extent[dim] // blocks).reshape((-1,) + (1,) * (len(extent) - 1 - dim))
    return gain


def gaussian(stream_key, dims, spread, limit, shards=(), held_as=jnp.bfloat16):
    values = spread * jax.random.normal(stream_key, dims, jnp.float32)
    if shards:
        values = values * block_scale(stream_key, dims, shards, -0.22, 0.18)
    return jnp.clip(values, -limit, limit).astype(held_as)


def setup_inputs(seed: int = 0) -> dict:
    keys = jax.random.split(jax.random.key(seed), 5)
    section_inputs = gaussian(keys[0], (N_SECTION, ALL_ROWS, D_IN), 1.0, 6.0, ((0, 4), (1, 32)))
    weights = gaussian(keys[1], (N_SECTION, D_IN, D_OUT), D_OUT ** -0.5, 0.109375, ((0, 4),))
    output_grads = gaussian(keys[2], (N_SECTION, ALL_ROWS, D_OUT), 0.5, 3.0, ((0, 4), (1, 32)))
    warm_start = gaussian(keys[3], (N_SECTION, RANK, D_OUT), D_OUT ** -0.5, 0.109375, ((0, 4),))
    return dict(section_inputs=section_inputs, weights=weights, output_grads=output_grads, warm_start=warm_start)


def orthonormal(matrix):
    result = []
    for position in range(matrix.shape[0]):
        column = matrix[position]
        for earlier in result:
            column = column - jnp.sum(earlier * column) * earlier
        column = column * lax.rsqrt(jnp.sum(column * column) + 1e-06)
        result.append(column)
    return jnp.stack(result)

def one_section(operands):
    section_inputs, weights, output_grads, warm_start = operands
    incoming = lax.dot_general(output_grads, weights, (((1,), (1,)), ((), ())), preferred_element_type=jnp.float32).astype(jnp.bfloat16)
    projected = lax.dot_general(warm_start, output_grads, (((1,), (1,)), ((), ())), preferred_element_type=jnp.float32)
    inputs_wide = section_inputs.astype(jnp.float32)
    grads_wide = output_grads.astype(jnp.float32)
    left_factor = jnp.dot(projected, inputs_wide, precision=lax.Precision.HIGHEST, preferred_element_type=jnp.float32) / N_DP
    basis = orthonormal(left_factor)
    backward = lax.dot_general(basis, inputs_wide, (((1,), (1,)), ((), ())), precision=lax.Precision.HIGHEST, preferred_element_type=jnp.float32)
    right_factor = jnp.dot(backward, grads_wide, precision=lax.Precision.HIGHEST, preferred_element_type=jnp.float32) / N_DP
    return (incoming, left_factor, right_factor)

def reference(section_inputs, weights, output_grads, warm_start):
    incoming, left_factor, right_factor = lax.map(one_section, (section_inputs, weights, output_grads, warm_start))
    arrived = jnp.concatenate([incoming[1:], jnp.zeros_like(incoming[:1])], axis=0)
    return (arrived, left_factor, right_factor)
```

```python
import functools

import jax
import jax.numpy as jnp
from jax import lax
from jax.experimental import pallas as pl
from jax.experimental.pallas import tpu as pltpu
from jax.sharding import PartitionSpec as P

TOKENS = 384
D_IN = 3072
D_OUT = 3072
RANK = 8
REPLICAS = 32
SECTIONS = 4
ROW_PARTS = 3
CHUNK = 512
PARTS = ((512, 512), (1024, 0), (1024, 0))

VMEM = pltpu.VMEM
F32 = jnp.float32
BF16 = jnp.bfloat16

NT = (((1,), (1,)), ((), ()))
NN = (((1,), (0,)), ((), ()))


def stacked(value):
    high = value.astype(BF16)
    rest = value - high.astype(F32)
    middle = rest.astype(BF16)
    low = (rest - middle.astype(F32)).astype(BF16)
    return jnp.concatenate([high, middle, low], axis=0)


def folded(value):
    return value[:RANK] + (value[RANK : 2 * RANK] + value[2 * RANK :])


def in_vmem(value):
    return pltpu.with_memory_space_constraint(value, VMEM)


def in_hbm(value):
    return pltpu.with_memory_space_constraint(value, pltpu.HBM)


def whole():
    return pl.BlockSpec(memory_space=VMEM)


def anywhere():
    return pl.BlockSpec(memory_space=pl.ANY)


def first_kernel(
    warm_hbm, grads_hbm, inputs_hbm, weight_hbm,
    partial_ref, grads_ref, inputs_ref, ahead_ref, warm_ref, sems,
):
    rows = TOKENS // ROW_PARTS
    warm_copy = pltpu.make_async_copy(warm_hbm, warm_ref, sems.at[0])
    warm_copy.start()
    copies = []
    for part in range(ROW_PARTS):
        span = pl.ds(part * rows, rows)
        copies.append(
            (
                pltpu.make_async_copy(
                    grads_hbm.at[span], grads_ref.at[span], sems.at[2 + 2 * part]
                ),
                pltpu.make_async_copy(
                    inputs_hbm.at[span], inputs_ref.at[span], sems.at[3 + 2 * part]
                ),
            )
        )
    for pair in copies:
        for copy in pair:
            copy.start()
    ahead_copy = pltpu.make_async_copy(weight_hbm.at[pl.ds(0, PARTS[0][0])], ahead_ref, sems.at[1])
    ahead_copy.start()
    warm_copy.wait()
    total = None
    for part in range(ROW_PARTS):
        span = slice(part * rows, (part + 1) * rows)
        copies[part][0].wait()
        projected = stacked(
            lax.dot_general(warm_ref[...], grads_ref[span, :], NT, preferred_element_type=F32)
        )
        copies[part][1].wait()
        term = lax.dot_general(
            projected, inputs_ref[span, :], NN, preferred_element_type=F32
        )
        total = term if total is None else total + term
    partial_ref[...] = folded(total)
    ahead_copy.wait()


def first_products(warm, grads, inputs, weight):
    return pl.pallas_call(
        first_kernel,
        out_shape=(
            VMEM((RANK, D_IN), F32),
            VMEM((TOKENS, D_OUT), BF16),
            VMEM((TOKENS, D_IN), BF16),
            VMEM((PARTS[0][0], D_OUT), BF16),
        ),
        in_specs=[anywhere()] * 4,
        out_specs=(whole(),) * 4,
        scratch_shapes=[
            VMEM((RANK, D_OUT), BF16),
            pltpu.SemaphoreType.DMA((2 + 2 * ROW_PARTS,)),
        ],
        compiler_params=pltpu.CompilerParams(vmem_limit_bytes=16 * 2**20),
        cost_estimate=pl.CostEstimate(
            flops=2 * 64 * TOKENS * D_IN, bytes_accessed=2 * TOKENS * D_IN * 2, transcendentals=0
        ),
        name="first_products",
    )(in_hbm(warm), in_hbm(grads), in_hbm(inputs), in_hbm(weight))


def second_kernel(own_ref, a_ref, b_ref, c_ref, grads_ref, inputs_ref, sum_ref, partial_ref):
    total = (own_ref[...] + a_ref[...]) + (b_ref[...] + c_ref[...])
    sum_ref[...] = total
    backward = folded(
        lax.dot_general(stacked(total), inputs_ref[...], NT, preferred_element_type=F32)
    )
    partial_ref[...] = folded(
        lax.dot_general(stacked(backward), grads_ref[...], NN, preferred_element_type=F32)
    )


def second_products(pieces, grads, inputs):
    return pl.pallas_call(
        second_kernel,
        out_shape=(VMEM((RANK, D_IN), F32), VMEM((RANK, D_OUT), F32)),
        in_specs=[whole()] * 6,
        out_specs=(whole(), whole()),
        compiler_params=pltpu.CompilerParams(vmem_limit_bytes=16 * 2**20),
        cost_estimate=pl.CostEstimate(
            flops=2 * 64 * TOKENS * D_IN, bytes_accessed=RANK * D_IN * 24, transcendentals=0
        ),
        name="second_products",
    )(*[in_vmem(piece) for piece in pieces], in_vmem(grads), in_vmem(inputs))


def gram_schmidt_kernel(sum_ref, left_ref, steps_ref):
    rows = sum_ref[...] * (1.0 / REPLICAS)
    left_ref[...] = rows
    place = lax.broadcasted_iota(jnp.int32, (RANK, 1), 0)
    lane = lax.broadcasted_iota(jnp.int32, (RANK, 128), 1)
    steps = (lax.broadcasted_iota(jnp.int32, (RANK, 128), 0) == lane).astype(F32)
    for rank in range(RANK):
        row = rows[rank : rank + 1]
        step = steps[rank : rank + 1]
        scale = lax.rsqrt(jnp.sum(row * row, axis=1, keepdims=True) + 1e-06)
        row = row * scale
        step = step * scale
        along = jnp.sum(rows * row, axis=1, keepdims=True)
        along = jnp.where(place > rank, along, 0.0)
        rows = rows - along * row
        steps = jnp.where(place == rank, step, steps - along * step)
    steps_ref[...] = steps


def gram_schmidt(total):
    return pl.pallas_call(
        gram_schmidt_kernel,
        out_shape=(
            jax.ShapeDtypeStruct((RANK, D_IN), F32),
            VMEM((RANK, 128), F32),
        ),
        in_specs=[whole()],
        out_specs=(whole(), whole()),
        compiler_params=pltpu.CompilerParams(vmem_limit_bytes=8 * 2**20),
        cost_estimate=pl.CostEstimate(
            flops=64 * RANK * D_IN, bytes_accessed=RANK * D_IN * 8, transcendentals=RANK
        ),
        name="gram_schmidt",
    )(in_vmem(total))


def last_kernel(own_ref, other_ref, steps_ref, right_ref):
    total = (own_ref[...] + other_ref[...]) * (1.0 / REPLICAS**2)
    steps = steps_ref[...]
    result = steps[:, :1] * total[:1]
    for rank in range(1, RANK):
        result = result + steps[:, rank : rank + 1] * total[rank : rank + 1]
    right_ref[...] = result


def last_step(own, other, steps):
    return pl.pallas_call(
        last_kernel,
        out_shape=jax.ShapeDtypeStruct((RANK, D_OUT), F32),
        in_specs=[whole()] * 3,
        out_specs=whole(),
        compiler_params=pltpu.CompilerParams(vmem_limit_bytes=8 * 2**20),
        name="last_step",
    )(in_vmem(own), in_vmem(other), in_vmem(steps))


def product_kernel(base, sizes, ahead, grads_ref, held_ref, weight_hbm, out_ref, *refs):
    held, streamed = sizes
    if ahead:
        ahead_ref, refs = refs[0], refs[1:]
    sems = refs[-1]
    if streamed:
        block_ref = refs[0]
        stream = pltpu.make_async_copy(
            weight_hbm.at[pl.ds(base + held, streamed)], block_ref, sems.at[0]
        )
        stream.start()
    if ahead:
        following = pltpu.make_async_copy(
            weight_hbm.at[pl.ds(base + held + streamed, ahead)], ahead_ref, sems.at[1]
        )
        following.start()

    def product(block_ref, rows, column):
        for row in range(0, rows, CHUNK):
            out_ref[:, column + row : column + row + CHUNK] = lax.dot_general(
                grads_ref[...], block_ref[row : row + CHUNK, :], NT, preferred_element_type=F32
            ).astype(BF16)

    product(held_ref, held, 0)
    if streamed:
        stream.wait()
        product(block_ref, streamed, held)
    if ahead:
        following.wait()


def product_part(grads, held, weight, part):
    sizes = PARTS[part]
    ahead = PARTS[part + 1][0] if part + 1 < len(PARTS) else 0
    base = sum(sum(earlier) for earlier in PARTS[:part])
    out_shape = [VMEM((TOKENS, sum(sizes)), BF16)]
    if ahead:
        out_shape.append(VMEM((ahead, D_OUT), BF16))
    scratch = [pltpu.SemaphoreType.DMA((2,))]
    if sizes[1]:
        scratch.insert(0, VMEM((sizes[1], D_OUT), BF16))
    return pl.pallas_call(
        functools.partial(product_kernel, base, sizes, ahead),
        out_shape=out_shape,
        in_specs=[whole(), whole(), anywhere()],
        out_specs=[whole()] * len(out_shape),
        scratch_shapes=scratch,
        compiler_params=pltpu.CompilerParams(vmem_limit_bytes=24 * 2**20),
        cost_estimate=pl.CostEstimate(
            flops=2 * TOKENS * D_OUT * sum(sizes),
            bytes_accessed=sum(sizes) * D_OUT * 2,
            transcendentals=0,
        ),
        name="product_part",
    )(in_vmem(grads), in_vmem(held), in_hbm(weight))


def store_kernel(*refs):
    *pieces, out_hbm, zeros_ref, sems = refs

    def moved(sources):
        base = 0
        copies = []
        for place, source in enumerate(sources):
            width = source.shape[1]
            copies.append(
                pltpu.make_async_copy(source, out_hbm.at[:, pl.ds(base, width)], sems.at[place])
            )
            base += width
        for copy in copies:
            copy.start()
        for copy in copies:
            copy.wait()

    last = lax.axis_index("section") == SECTIONS - 1

    @pl.when(last)
    def _():
        zeros_ref[...] = jnp.zeros_like(zeros_ref)
        moved([zeros_ref] * (D_IN // CHUNK))

    @pl.when(jnp.logical_not(last))
    def _():
        moved(pieces)


def stored(pieces):
    return pl.pallas_call(
        store_kernel,
        out_shape=jax.ShapeDtypeStruct((TOKENS, D_IN), BF16),
        in_specs=[whole()] * len(pieces),
        out_specs=anywhere(),
        scratch_shapes=[
            VMEM((TOKENS, CHUNK), BF16),
            pltpu.SemaphoreType.DMA((D_IN // CHUNK,)),
        ],
        compiler_params=pltpu.CompilerParams(vmem_limit_bytes=8 * 2**20),
        cost_estimate=pl.CostEstimate(
            flops=0, bytes_accessed=4 * TOKENS * D_IN, transcendentals=0
        ),
        name="store",
    )(*[in_vmem(piece) for piece in pieces])


def replica(y, x, z):
    return (y % 4) * 8 + (x % 2) * 4 + z % 4


def moves(dy, dx, dz):
    return [
        (replica(y, x, z), replica(y + dy, x + dx, z + dz))
        for y in range(4)
        for x in range(2)
        for z in range(4)
    ]


X_ROUND = [moves(0, 1, 0)]
Y_ROUND = [moves(k, 0, 0) for k in (1, 3, 2)]
Z_ROUND = [moves(0, 0, k) for k in (1, 3, 2)]


def sent(value, pattern):
    return [lax.ppermute(value, "dp", pairs) for pairs in pattern]


def tied(*values):
    return lax.optimization_barrier(values)


def handed(piece):
    return lax.ppermute(piece, "section", [(1, 0), (2, 1), (3, 2), (0, 3)])


def per_device(section_inputs, weights, output_grads, warm_start):
    weight = weights[0]
    value, grads, inputs, held = first_products(
        warm_start[0], output_grads[0], section_inputs[0], weight
    )

    arrivals = sent(value, X_ROUND)
    piece, held = product_part(grads, held, weight, 0)
    first = handed(piece)
    value = value + arrivals[0]

    value, held = tied(value, held)
    arrivals = sent(value, Y_ROUND)
    piece, held = product_part(grads, held, weight, 1)
    second = handed(piece)
    value = (value + arrivals[0]) + (arrivals[1] + arrivals[2])

    value, held = tied(value, held)
    arrivals = sent(value, Z_ROUND)
    (piece,) = product_part(grads, held, weight, 2)
    third = handed(piece)
    *pieces, first, _ = tied(value, *arrivals, first, piece)
    total, value = second_products(pieces, grads, inputs)

    arrivals = sent(value, Z_ROUND)
    tied_total, _ = tied(total, value)
    left_factor, steps = gram_schmidt(tied_total)
    value = (value + arrivals[0]) + (arrivals[1] + arrivals[2])
    value, steps, second = tied(value, steps, second)
    arrivals = sent(value, Y_ROUND)
    value = (value + arrivals[0]) + (arrivals[1] + arrivals[2])
    value, first, second, third = tied(value, first, second, third)
    arrivals = sent(value, X_ROUND)
    arrived = stored([first, second, third])
    right_factor = last_step(value, arrivals[0], steps)
    return (arrived[None], left_factor[None], right_factor[None])


def solution(mesh):
    return jax.shard_map(
        per_device,
        mesh=mesh,
        in_specs=(
            P("section", "dp", None),
            P("section", None, None),
            P("section", "dp", None),
            P("section", None, None),
        ),
        out_specs=(P("section", "dp", None), P("section", None, None), P("section", None, None)),
        check_vma=False,
    )
```

```python
import functools

import jax
import jax.numpy as jnp
from jax import lax
from jax.experimental import pallas as pl
from jax.experimental.pallas import tpu as pltpu
from jax.sharding import PartitionSpec as P

TOKENS = 384
D_IN = 3072
D_OUT = 3072
RANK = 8
REPLICAS = 32
SECTIONS = 4
ROW_PARTS = 3
WINDOW = 4
WIRE = jnp.bfloat16
CHUNK = 512
PARTS = ((512, 512), (1024, 0), (1024, 0))

VMEM = pltpu.VMEM
F32 = jnp.float32
BF16 = jnp.bfloat16

NT = (((1,), (1,)), ((), ()))
NN = (((1,), (0,)), ((), ()))


def stacked(value):
    high = value.astype(BF16)
    rest = value - high.astype(F32)
    middle = rest.astype(BF16)
    low = (rest - middle.astype(F32)).astype(BF16)
    return jnp.concatenate([high, middle, low], axis=0)


def folded(value):
    return value[:RANK] + (value[RANK : 2 * RANK] + value[2 * RANK :])


def in_vmem(value):
    return pltpu.with_memory_space_constraint(value, VMEM)


def in_hbm(value):
    return pltpu.with_memory_space_constraint(value, pltpu.HBM)


def whole():
    return pl.BlockSpec(memory_space=VMEM)


def anywhere():
    return pl.BlockSpec(memory_space=pl.ANY)


def first_kernel(
    warm_hbm, grads_hbm, inputs_hbm, weight_hbm, partial_ref, grads_ref, inputs_ref, *refs
):
    ahead = PARTS[0][0]
    if ahead:
        ahead_ref, refs = refs[0], refs[1:]
    warm_ref, sems = refs
    rows = TOKENS // ROW_PARTS
    warm_copy = pltpu.make_async_copy(warm_hbm, warm_ref, sems.at[0])
    warm_copy.start()
    copies = []
    for part in range(ROW_PARTS):
        span = pl.ds(part * rows, rows)
        copies.append(
            (
                pltpu.make_async_copy(
                    grads_hbm.at[span], grads_ref.at[span], sems.at[2 + 2 * part]
                ),
                pltpu.make_async_copy(
                    inputs_hbm.at[span], inputs_ref.at[span], sems.at[3 + 2 * part]
                ),
            )
        )
    if ahead:
        ahead_copy = pltpu.make_async_copy(
            weight_hbm.at[pl.ds(0, ahead)], ahead_ref, sems.at[1]
        )

    def start(part):
        if part < ROW_PARTS:
            for copy in copies[part]:
                copy.start()
        elif ahead and part == ROW_PARTS:
            ahead_copy.start()

    for part in range(WINDOW):
        start(part)
    warm_copy.wait()
    total = None
    for part in range(ROW_PARTS):
        span = slice(part * rows, (part + 1) * rows)
        copies[part][0].wait()
        start(part + WINDOW)
        projected = stacked(
            lax.dot_general(warm_ref[...], grads_ref[span, :], NT, preferred_element_type=F32)
        )
        copies[part][1].wait()
        term = lax.dot_general(
            projected, inputs_ref[span, :], NN, preferred_element_type=F32
        )
        total = term if total is None else total + term
    partial_ref[...] = folded(total)
    if ahead:
        ahead_copy.wait()


def first_products(warm, grads, inputs, weight):
    ahead = PARTS[0][0]
    out_shape = [
        VMEM((RANK, D_IN), F32),
        VMEM((TOKENS, D_OUT), BF16),
        VMEM((TOKENS, D_IN), BF16),
    ]
    if ahead:
        out_shape.append(VMEM((ahead, D_OUT), BF16))
    results = pl.pallas_call(
        first_kernel,
        out_shape=out_shape,
        in_specs=[anywhere()] * 4,
        out_specs=[whole()] * len(out_shape),
        scratch_shapes=[
            VMEM((RANK, D_OUT), BF16),
            pltpu.SemaphoreType.DMA((2 + 2 * ROW_PARTS,)),
        ],
        compiler_params=pltpu.CompilerParams(vmem_limit_bytes=16 * 2**20),
        cost_estimate=pl.CostEstimate(
            flops=2 * 64 * TOKENS * D_IN, bytes_accessed=2 * TOKENS * D_IN * 2, transcendentals=0
        ),
        name="first_products",
    )(in_hbm(warm), in_hbm(grads), in_hbm(inputs), in_hbm(weight))
    return list(results) if ahead else [*results, None]


def gram_schmidt_steps(rows):
    place = lax.broadcasted_iota(jnp.int32, (RANK, 1), 0)
    lane = lax.broadcasted_iota(jnp.int32, (RANK, 128), 1)
    steps = (lax.broadcasted_iota(jnp.int32, (RANK, 128), 0) == lane).astype(F32)
    for rank in range(RANK):
        row = rows[rank : rank + 1]
        step = steps[rank : rank + 1]
        scale = lax.rsqrt(jnp.sum(row * row, axis=1, keepdims=True) + 1e-06)
        row = row * scale
        step = step * scale
        along = jnp.sum(rows * row, axis=1, keepdims=True)
        along = jnp.where(place > rank, along, 0.0)
        rows = rows - along * row
        steps = jnp.where(place == rank, step, steps - along * step)
    return steps


def applied(steps, value):
    result = steps[:, :1] * value[:1]
    for rank in range(1, RANK):
        result = result + steps[:, rank : rank + 1] * value[rank : rank + 1]
    return result


def second_kernel(own_ref, a_ref, b_ref, c_ref, grads_ref, inputs_ref, left_ref, partial_ref):
    total = (own_ref[...] + a_ref[...]) + (b_ref[...] + c_ref[...])
    total = total * (1.0 / REPLICAS)
    left_ref[...] = total
    steps = gram_schmidt_steps(total)
    backward = folded(
        lax.dot_general(stacked(total), inputs_ref[...], NT, preferred_element_type=F32)
    )
    partial_value = folded(
        lax.dot_general(stacked(backward), grads_ref[...], NN, preferred_element_type=F32)
    )
    partial_ref[...] = (applied(steps, partial_value) * (1.0 / REPLICAS)).astype(
        partial_ref.dtype
    )


def second_products(pieces, grads, inputs):
    return pl.pallas_call(
        second_kernel,
        out_shape=(VMEM((RANK, D_IN), F32), VMEM((RANK, D_OUT), WIRE)),
        in_specs=[whole()] * 6,
        out_specs=(whole(), whole()),
        compiler_params=pltpu.CompilerParams(vmem_limit_bytes=16 * 2**20),
        cost_estimate=pl.CostEstimate(
            flops=2 * 64 * TOKENS * D_IN, bytes_accessed=RANK * D_IN * 24, transcendentals=0
        ),
        name="second_products",
    )(*[in_vmem(piece) for piece in pieces], in_vmem(grads), in_vmem(inputs))


def left_kernel(left_ref, out_hbm, sem):
    copy = pltpu.make_async_copy(left_ref, out_hbm, sem)
    copy.start()
    copy.wait()


def left_stored(left):
    return pl.pallas_call(
        left_kernel,
        out_shape=jax.ShapeDtypeStruct((RANK, D_IN), F32),
        in_specs=[whole()],
        out_specs=anywhere(),
        scratch_shapes=[pltpu.SemaphoreType.DMA],
        compiler_params=pltpu.CompilerParams(vmem_limit_bytes=2 * 2**20),
        name="left_stored",
    )(in_vmem(left))


def widened(*values):
    values = [value.astype(F32) for value in values]
    return functools.reduce(lambda left, right: left + right, values)


def product_kernel(base, sizes, ahead, grads_ref, *refs):
    held, streamed = sizes
    if held:
        held_ref, refs = refs[0], refs[1:]
    weight_hbm, out_ref, *refs = refs
    if ahead:
        ahead_ref, refs = refs[0], refs[1:]
    sems = refs[-1]
    streams = []
    for row in range(0, streamed, CHUNK):
        streams.append(
            pltpu.make_async_copy(
                weight_hbm.at[pl.ds(base + held + row, CHUNK)],
                refs[0].at[pl.ds(row, CHUNK)],
                sems.at[1 + row // CHUNK],
            )
        )
    for stream in streams:
        stream.start()
    if ahead:
        following = pltpu.make_async_copy(
            weight_hbm.at[pl.ds(base + held + streamed, ahead)], ahead_ref, sems.at[0]
        )
        following.start()

    def product(block_ref, row, column):
        out_ref[:, column : column + CHUNK] = lax.dot_general(
            grads_ref[...], block_ref[row : row + CHUNK, :], NT, preferred_element_type=F32
        ).astype(BF16)

    for row in range(0, held, CHUNK):
        product(held_ref, row, row)
    for row in range(0, streamed, CHUNK):
        streams[row // CHUNK].wait()
        product(refs[0], row, held + row)
    if ahead:
        following.wait()


def product_part(grads, held, weight, part):
    sizes = PARTS[part]
    ahead = PARTS[part + 1][0] if part + 1 < len(PARTS) else 0
    base = sum(sum(earlier) for earlier in PARTS[:part])
    operands = [in_vmem(grads)]
    if sizes[0]:
        operands.append(in_vmem(held))
    operands.append(in_hbm(weight))
    out_shape = [VMEM((TOKENS, sum(sizes)), BF16)]
    if ahead:
        out_shape.append(VMEM((ahead, D_OUT), BF16))
    scratch = [pltpu.SemaphoreType.DMA((1 + D_IN // CHUNK,))]
    if sizes[1]:
        scratch.insert(0, VMEM((sizes[1], D_OUT), BF16))
    return pl.pallas_call(
        functools.partial(product_kernel, base, sizes, ahead),
        out_shape=out_shape,
        in_specs=[whole()] * (len(operands) - 1) + [anywhere()],
        out_specs=[whole()] * len(out_shape),
        scratch_shapes=scratch,
        compiler_params=pltpu.CompilerParams(vmem_limit_bytes=32 * 2**20),
        cost_estimate=pl.CostEstimate(
            flops=2 * TOKENS * D_OUT * sum(sizes),
            bytes_accessed=sum(sizes) * D_OUT * 2,
            transcendentals=0,
        ),
        name="product_part",
    )(*operands)


def store_kernel(*refs):
    *pieces, out_hbm, zeros_ref, sems = refs

    def moved(sources):
        base = 0
        copies = []
        for place, source in enumerate(sources):
            width = source.shape[1]
            copies.append(
                pltpu.make_async_copy(source, out_hbm.at[:, pl.ds(base, width)], sems.at[place])
            )
            base += width
        for copy in copies:
            copy.start()
        for copy in copies:
            copy.wait()

    last = lax.axis_index("section") == SECTIONS - 1

    @pl.when(last)
    def _():
        zeros_ref[...] = jnp.zeros_like(zeros_ref)
        moved([zeros_ref] * (D_IN // CHUNK))

    @pl.when(jnp.logical_not(last))
    def _():
        moved(pieces)


def stored(pieces):
    return pl.pallas_call(
        store_kernel,
        out_shape=jax.ShapeDtypeStruct((TOKENS, D_IN), BF16),
        in_specs=[whole()] * len(pieces),
        out_specs=anywhere(),
        scratch_shapes=[
            VMEM((TOKENS, CHUNK), BF16),
            pltpu.SemaphoreType.DMA((D_IN // CHUNK,)),
        ],
        compiler_params=pltpu.CompilerParams(vmem_limit_bytes=8 * 2**20),
        cost_estimate=pl.CostEstimate(
            flops=0, bytes_accessed=4 * TOKENS * D_IN, transcendentals=0
        ),
        name="store",
    )(*[in_vmem(piece) for piece in pieces])


def replica(y, x, z):
    return (y % 4) * 8 + (x % 2) * 4 + z % 4


def moves(dy, dx, dz):
    return [
        (replica(y, x, z), replica(y + dy, x + dx, z + dz))
        for y in range(4)
        for x in range(2)
        for z in range(4)
    ]


def swaps(axis, masks):
    patterns = []
    for mask in masks:
        flip = [0, 0, 0]
        flip[axis] = mask
        patterns.append(
            [
                (replica(y, x, z), replica(y ^ flip[0], x ^ flip[1], z ^ flip[2]))
                for y in range(4)
                for x in range(2)
                for z in range(4)
            ]
        )
    return patterns


def ring(axis, steps):
    patterns = []
    for step in steps:
        shift = [0, 0, 0]
        shift[axis] = step
        patterns.append(moves(*shift))
    return patterns


X_ROUND = ring(1, (1,))
LEFT_Y_ROUND = swaps(0, (1, 3, 2))
LEFT_Z_ROUND = swaps(2, (1, 3, 2))
RIGHT_Z_ROUND = swaps(2, (1, 3, 2))
RIGHT_Y_ROUND = swaps(0, (1, 3, 2))


def sent(value, pattern):
    return [lax.ppermute(value, "dp", pairs) for pairs in pattern]


def tied(*values):
    return lax.optimization_barrier(values)


def handed(piece):
    return lax.ppermute(piece, "section", [(1, 0), (2, 1), (3, 2), (0, 3)])


def per_device(section_inputs, weights, output_grads, warm_start):
    weight = weights[0]
    value, grads, inputs, held = first_products(
        warm_start[0], output_grads[0], section_inputs[0], weight
    )

    arrivals = sent(value, X_ROUND)
    piece, held = product_part(grads, held, weight, 0)
    first = handed(piece)
    value = value + arrivals[0]

    value, held = tied(value, held)
    arrivals = sent(value, LEFT_Y_ROUND)
    piece, held = product_part(grads, held, weight, 1)
    second = handed(piece)
    value = (value + arrivals[0]) + (arrivals[1] + arrivals[2])

    value, held = tied(value, held)
    arrivals = sent(value, LEFT_Z_ROUND)
    (piece,) = product_part(grads, held, weight, 2)
    third = handed(piece)
    *pieces, first, _ = tied(value, *arrivals, first, piece)
    left, value = second_products(pieces, grads, inputs)

    arrivals = sent(value, RIGHT_Z_ROUND)
    tied_left, _ = tied(left, value)
    left_factor = left_stored(tied_left)
    value = widened(value, *arrivals).astype(WIRE)
    value, left_factor, second = tied(value, left_factor, second)
    arrivals = sent(value, RIGHT_Y_ROUND)
    value = widened(value, *arrivals)
    value, first, second, third = tied(value, first, second, third)
    value = value.astype(WIRE)
    arrivals = sent(value, X_ROUND)
    arrived = stored([first, second, third])
    right_factor = widened(value, *arrivals)
    return (arrived[None], left_factor[None], right_factor[None])


def solution(mesh):
    return jax.shard_map(
        per_device,
        mesh=mesh,
        in_specs=(
            P("section", "dp", None),
            P("section", None, None),
            P("section", "dp", None),
            P("section", None, None),
        ),
        out_specs=(P("section", "dp", None), P("section", None, None), P("section", None, None)),
        check_vma=False,
    )
```

```python
import functools

import jax
import jax.numpy as jnp
from jax import lax
from jax.experimental import pallas as pl
from jax.experimental.pallas import tpu as pltpu
from jax.sharding import PartitionSpec as P

TOKENS = 384
D_IN = 3072
D_OUT = 3072
RANK = 8
REPLICAS = 32
SECTIONS = 4
ROW_PARTS = (128, 128, 128)
WIRE = jnp.bfloat16
CHUNK = 512
SHARE = 4
PARTS = ((512, 512), (1024, 0), (1024, 0))

VMEM = pltpu.VMEM
F32 = jnp.float32
BF16 = jnp.bfloat16

NT = (((1,), (1,)), ((), ()))
NN = (((1,), (0,)), ((), ()))


def stacked(value):
    high = value.astype(BF16)
    rest = value - high.astype(F32)
    middle = rest.astype(BF16)
    low = (rest - middle.astype(F32)).astype(BF16)
    return jnp.concatenate([high, middle, low], axis=0)


def folded(value):
    return value[:RANK] + (value[RANK : 2 * RANK] + value[2 * RANK :])


def in_vmem(value):
    return pltpu.with_memory_space_constraint(value, VMEM)


def in_hbm(value):
    return pltpu.with_memory_space_constraint(value, pltpu.HBM)


def whole():
    return pl.BlockSpec(memory_space=VMEM)


def anywhere():
    return pl.BlockSpec(memory_space=pl.ANY)


def first_kernel(
    warm_hbm, grads_hbm, inputs_hbm, weight_hbm, partial_ref, grads_ref, inputs_ref, *refs
):
    ahead = PARTS[0][0]
    if ahead:
        ahead_ref, refs = refs[0], refs[1:]
    warm_ref, sems = refs
    warm_copy = pltpu.make_async_copy(warm_hbm, warm_ref, sems.at[0])
    warm_copy.start()
    spans = []
    copies = []
    first = 0
    for part, rows in enumerate(ROW_PARTS):
        span = pl.ds(first, rows)
        copies.append(
            (
                pltpu.make_async_copy(
                    grads_hbm.at[span], grads_ref.at[span], sems.at[2 + 2 * part]
                ),
                pltpu.make_async_copy(
                    inputs_hbm.at[span], inputs_ref.at[span], sems.at[3 + 2 * part]
                ),
            )
        )
        spans.append(slice(first, first + rows))
        first += rows
    for pair in copies:
        for copy in pair:
            copy.start()
    if ahead:
        ahead_copy = pltpu.make_async_copy(
            weight_hbm.at[pl.ds(0, ahead)], ahead_ref, sems.at[1]
        )
        ahead_copy.start()
    warm_copy.wait()
    total = None
    for span, (grads_copy, inputs_copy) in zip(spans, copies):
        grads_copy.wait()
        projected = stacked(
            lax.dot_general(warm_ref[...], grads_ref[span, :], NT, preferred_element_type=F32)
        )
        inputs_copy.wait()
        term = lax.dot_general(
            projected, inputs_ref[span, :], NN, preferred_element_type=F32
        )
        total = term if total is None else total + term
    partial_ref[...] = folded(total)
    if ahead:
        ahead_copy.wait()


def first_products(warm, grads, inputs, weight):
    ahead = PARTS[0][0]
    out_shape = [
        VMEM((RANK, D_IN), F32),
        VMEM((TOKENS, D_OUT), BF16),
        VMEM((TOKENS, D_IN), BF16),
    ]
    if ahead:
        out_shape.append(VMEM((ahead, D_OUT), BF16))
    results = pl.pallas_call(
        first_kernel,
        out_shape=out_shape,
        in_specs=[anywhere()] * 4,
        out_specs=[whole()] * len(out_shape),
        scratch_shapes=[
            VMEM((RANK, D_OUT), BF16),
            pltpu.SemaphoreType.DMA((2 + 2 * len(ROW_PARTS),)),
        ],
        compiler_params=pltpu.CompilerParams(vmem_limit_bytes=16 * 2**20),
        cost_estimate=pl.CostEstimate(
            flops=2 * 64 * TOKENS * D_IN, bytes_accessed=2 * TOKENS * D_IN * 2, transcendentals=0
        ),
        name="first_products",
    )(in_hbm(warm), in_hbm(grads), in_hbm(inputs), in_hbm(weight))
    return list(results) if ahead else [*results, None]


def gram_schmidt_steps(rows):
    place = lax.broadcasted_iota(jnp.int32, (RANK, 1), 0)
    lane = lax.broadcasted_iota(jnp.int32, (RANK, 128), 1)
    steps = (lax.broadcasted_iota(jnp.int32, (RANK, 128), 0) == lane).astype(F32)
    for rank in range(RANK):
        row = rows[rank : rank + 1]
        step = steps[rank : rank + 1]
        scale = lax.rsqrt(jnp.sum(row * row, axis=1, keepdims=True) + 1e-06)
        row = row * scale
        step = step * scale
        along = jnp.sum(rows * row, axis=1, keepdims=True)
        along = jnp.where(place > rank, along, 0.0)
        rows = rows - along * row
        steps = jnp.where(place == rank, step, steps - along * step)
    return steps


def applied(steps, value):
    result = steps[:, :1] * value[:1]
    for rank in range(1, RANK):
        result = result + steps[:, rank : rank + 1] * value[rank : rank + 1]
    return result


def second_kernel(*refs):
    *piece_refs, grads_ref, inputs_ref, left_ref, partial_ref = refs
    total = functools.reduce(lambda left, right: left + right, [ref[...] for ref in piece_refs])
    total = total * (1.0 / REPLICAS)
    left_ref[...] = total
    steps = gram_schmidt_steps(total)
    backward = folded(
        lax.dot_general(stacked(total), inputs_ref[...], NT, preferred_element_type=F32)
    )
    partial_value = folded(
        lax.dot_general(stacked(backward), grads_ref[...], NN, preferred_element_type=F32)
    )
    partial_ref[...] = (applied(steps, partial_value) * (1.0 / REPLICAS)).astype(
        partial_ref.dtype
    )


def second_products(pieces, grads, inputs):
    return pl.pallas_call(
        second_kernel,
        out_shape=(VMEM((RANK, D_IN), F32), VMEM((RANK, D_OUT), WIRE)),
        in_specs=[whole()] * (len(pieces) + 2),
        out_specs=(whole(), whole()),
        compiler_params=pltpu.CompilerParams(vmem_limit_bytes=16 * 2**20),
        cost_estimate=pl.CostEstimate(
            flops=2 * 64 * TOKENS * D_IN, bytes_accessed=RANK * D_IN * 24, transcendentals=0
        ),
        name="second_products",
    )(*[in_vmem(piece) for piece in pieces], in_vmem(grads), in_vmem(inputs))


def left_kernel(left_ref, out_hbm, sem):
    copy = pltpu.make_async_copy(left_ref, out_hbm, sem)
    copy.start()
    copy.wait()


def left_stored(left):
    return pl.pallas_call(
        left_kernel,
        out_shape=jax.ShapeDtypeStruct((RANK, D_IN), F32),
        in_specs=[whole()],
        out_specs=anywhere(),
        scratch_shapes=[pltpu.SemaphoreType.DMA],
        compiler_params=pltpu.CompilerParams(vmem_limit_bytes=2 * 2**20),
        name="left_stored",
    )(in_vmem(left))


def widened(*values):
    values = [value.astype(F32) for value in values]
    return functools.reduce(lambda left, right: left + right, values)


def product_kernel(base, sizes, ahead, grads_ref, *refs):
    held, streamed = sizes
    if held:
        held_ref, refs = refs[0], refs[1:]
    weight_hbm, out_ref, *refs = refs
    if ahead:
        ahead_ref, refs = refs[0], refs[1:]
    sems = refs[-1]
    streams = []
    for row in range(0, streamed, CHUNK):
        streams.append(
            pltpu.make_async_copy(
                weight_hbm.at[pl.ds(base + held + row, CHUNK)],
                refs[0].at[pl.ds(row, CHUNK)],
                sems.at[1 + row // CHUNK],
            )
        )
    for stream in streams:
        stream.start()
    if ahead:
        following = pltpu.make_async_copy(
            weight_hbm.at[pl.ds(base + held + streamed, ahead)], ahead_ref, sems.at[0]
        )
        following.start()

    def product(block_ref, row, column):
        out_ref[:, column : column + CHUNK] = lax.dot_general(
            grads_ref[...], block_ref[row : row + CHUNK, :], NT, preferred_element_type=F32
        ).astype(BF16)

    for row in range(0, held, CHUNK):
        product(held_ref, row, row)
    for row in range(0, streamed, CHUNK):
        streams[row // CHUNK].wait()
        product(refs[0], row, held + row)
    if ahead:
        following.wait()


def product_part(grads, held, weight, part):
    sizes = PARTS[part]
    ahead = PARTS[part + 1][0] if part + 1 < len(PARTS) else 0
    base = sum(sum(earlier) for earlier in PARTS[:part])
    operands = [in_vmem(grads)]
    if sizes[0]:
        operands.append(in_vmem(held))
    operands.append(in_hbm(weight))
    out_shape = [VMEM((TOKENS, sum(sizes)), BF16)]
    if ahead:
        out_shape.append(VMEM((ahead, D_OUT), BF16))
    scratch = [pltpu.SemaphoreType.DMA((1 + D_IN // CHUNK,))]
    if sizes[1]:
        scratch.insert(0, VMEM((sizes[1], D_OUT), BF16))
    return pl.pallas_call(
        functools.partial(product_kernel, base, sizes, ahead),
        out_shape=out_shape,
        in_specs=[whole()] * (len(operands) - 1) + [anywhere()],
        out_specs=[whole()] * len(out_shape),
        scratch_shapes=scratch,
        compiler_params=pltpu.CompilerParams(vmem_limit_bytes=32 * 2**20),
        cost_estimate=pl.CostEstimate(
            flops=2 * TOKENS * D_OUT * sum(sizes) // SHARE,
            bytes_accessed=sum(sizes) * D_OUT * 2 // SHARE,
            transcendentals=0,
        ),
        name="product_part",
    )(*operands)


def store_kernel(*refs):
    *pieces, out_hbm, zeros_ref, sems = refs

    def moved(sources):
        base = 0
        copies = []
        for place, source in enumerate(sources):
            width = source.shape[1]
            copies.append(
                pltpu.make_async_copy(source, out_hbm.at[:, pl.ds(base, width)], sems.at[place])
            )
            base += width
        for copy in copies:
            copy.start()
        for copy in copies:
            copy.wait()

    last = lax.axis_index("section") == SECTIONS - 1

    @pl.when(last)
    def _():
        zeros_ref[...] = jnp.zeros_like(zeros_ref)
        moved([zeros_ref] * (D_IN // CHUNK))

    @pl.when(jnp.logical_not(last))
    def _():
        moved(pieces)


def stored(pieces):
    return pl.pallas_call(
        store_kernel,
        out_shape=jax.ShapeDtypeStruct((TOKENS, D_IN), BF16),
        in_specs=[whole()] * len(pieces),
        out_specs=anywhere(),
        scratch_shapes=[
            VMEM((TOKENS, CHUNK), BF16),
            pltpu.SemaphoreType.DMA((D_IN // CHUNK,)),
        ],
        compiler_params=pltpu.CompilerParams(vmem_limit_bytes=8 * 2**20),
        cost_estimate=pl.CostEstimate(
            flops=0, bytes_accessed=4 * TOKENS * D_IN, transcendentals=0
        ),
        name="store",
    )(*[in_vmem(piece) for piece in pieces])


def replica(y, x, z):
    return (y % 4) * 8 + (x % 2) * 4 + z % 4


def moves(dy, dx, dz):
    return [
        (replica(y, x, z), replica(y + dy, x + dx, z + dz))
        for y in range(4)
        for x in range(2)
        for z in range(4)
    ]


def swaps(*masks):
    return [
        [
            (replica(y, x, z), replica(y ^ flip_y, x ^ flip_x, z ^ flip_z))
            for y in range(4)
            for x in range(2)
            for z in range(4)
        ]
        for flip_y, flip_x, flip_z in masks
    ]


X_ROUND = swaps((0, 1, 0))
Y_ROUND = swaps((1, 0, 0), (3, 0, 0), (2, 0, 0))
Z_ROUND = swaps((0, 0, 1), (0, 0, 3), (0, 0, 2))
LEFT_ROUNDS = [X_ROUND, Z_ROUND, Y_ROUND]
PART_OF_ROUND = {0: 0, 1: 1, 2: 2}
RIGHT_ROUNDS = [Z_ROUND, Y_ROUND, X_ROUND]


def sent(value, pattern):
    return [lax.ppermute(value, "dp", pairs) for pairs in pattern]


def tied(*values):
    return lax.optimization_barrier(values)


def handed(piece):
    return lax.ppermute(piece, "section", [(1, 0), (2, 1), (3, 2), (0, 3)])


def per_device(section_inputs, weights, output_grads, warm_start):
    weight = weights[0]
    value, grads, inputs, held = first_products(
        warm_start[0], output_grads[0], section_inputs[0], weight
    )

    arrived = []
    for place, pattern in enumerate(LEFT_ROUNDS):
        if place:
            value = widened(value, *arrivals)
            value, held = tied(value, held)
        arrivals = sent(value, pattern)
        part = PART_OF_ROUND.get(place)
        if part is not None:
            piece, *held = product_part(grads, held, weight, part)
            held = held[0] if held else piece
            arrived.append(handed(piece))
    *pieces, arrived[0], _ = tied(value, *arrivals, arrived[0], held)
    left, value = second_products(pieces, grads, inputs)

    for place, pattern in enumerate(RIGHT_ROUNDS):
        if place:
            value = widened(value, *arrivals).astype(WIRE)
        if place == len(RIGHT_ROUNDS) - 1:
            value, *arrived = tied(value, *arrived)
        elif place == 1:
            value, left_factor, *arrived[:-1] = tied(value, left_factor, *arrived[:-1])
        arrivals = sent(value, pattern)
        if not place:
            tied_left, _ = tied(left, value)
            left_factor = left_stored(tied_left)
    arrived = stored(arrived)
    right_factor = widened(value, *arrivals)
    return (arrived[None], left_factor[None], right_factor[None])


def solution(mesh):
    return jax.shard_map(
        per_device,
        mesh=mesh,
        in_specs=(
            P("section", "dp", None),
            P("section", None, None),
            P("section", "dp", None),
            P("section", None, None),
        ),
        out_specs=(P("section", "dp", None), P("section", None, None), P("section", None, None)),
        check_vma=False,
    )
```

```python
import functools

import jax
import jax.numpy as jnp
from jax import lax
from jax.experimental import pallas as pl
from jax.experimental.pallas import tpu as pltpu
from jax.sharding import PartitionSpec as P

TOKENS = 384
D_IN = 3072
D_OUT = 3072
RANK = 8
REPLICAS = 32
SECTIONS = 4
ROW_PARTS = (128, 128, 128)
WIRE = jnp.bfloat16
CHUNK = 512
SHARE = 4
PARTS = ((512, 512), (1024, 0), (1024, 0))

VMEM = pltpu.VMEM
F32 = jnp.float32
BF16 = jnp.bfloat16

NT = (((1,), (1,)), ((), ()))
NN = (((1,), (0,)), ((), ()))


def stacked(value):
    high = value.astype(BF16)
    rest = value - high.astype(F32)
    middle = rest.astype(BF16)
    low = (rest - middle.astype(F32)).astype(BF16)
    return jnp.concatenate([high, middle, low], axis=0)


def folded(value):
    return value[:RANK] + (value[RANK : 2 * RANK] + value[2 * RANK :])


def in_vmem(value):
    return pltpu.with_memory_space_constraint(value, VMEM)


def in_hbm(value):
    return pltpu.with_memory_space_constraint(value, pltpu.HBM)


def whole():
    return pl.BlockSpec(memory_space=VMEM)


def anywhere():
    return pl.BlockSpec(memory_space=pl.ANY)


def first_kernel(
    warm_hbm, grads_hbm, inputs_hbm, weight_hbm, partial_ref, grads_ref, inputs_ref, *refs
):
    ahead = PARTS[0][0]
    if ahead:
        ahead_ref, refs = refs[0], refs[1:]
    warm_ref, sems = refs
    warm_copy = pltpu.make_async_copy(warm_hbm, warm_ref, sems.at[0])
    warm_copy.start()
    spans = []
    copies = []
    first = 0
    for part, rows in enumerate(ROW_PARTS):
        span = pl.ds(first, rows)
        copies.append(
            (
                pltpu.make_async_copy(
                    grads_hbm.at[span], grads_ref.at[span], sems.at[2 + 2 * part]
                ),
                pltpu.make_async_copy(
                    inputs_hbm.at[span], inputs_ref.at[span], sems.at[3 + 2 * part]
                ),
            )
        )
        spans.append(slice(first, first + rows))
        first += rows
    for pair in copies:
        for copy in pair:
            copy.start()
    if ahead:
        ahead_copy = pltpu.make_async_copy(
            weight_hbm.at[pl.ds(0, ahead)], ahead_ref, sems.at[1]
        )
        ahead_copy.start()
    warm_copy.wait()
    total = None
    for span, (grads_copy, inputs_copy) in zip(spans, copies):
        grads_copy.wait()
        projected = stacked(
            lax.dot_general(warm_ref[...], grads_ref[span, :], NT, preferred_element_type=F32)
        )
        inputs_copy.wait()
        term = lax.dot_general(
            projected, inputs_ref[span, :], NN, preferred_element_type=F32
        )
        total = term if total is None else total + term
    partial_ref[...] = folded(total)
    if ahead:
        ahead_copy.wait()


def first_products(warm, grads, inputs, weight):
    ahead = PARTS[0][0]
    out_shape = [
        VMEM((RANK, D_IN), F32),
        VMEM((TOKENS, D_OUT), BF16),
        VMEM((TOKENS, D_IN), BF16),
    ]
    if ahead:
        out_shape.append(VMEM((ahead, D_OUT), BF16))
    results = pl.pallas_call(
        first_kernel,
        out_shape=out_shape,
        in_specs=[anywhere()] * 4,
        out_specs=[whole()] * len(out_shape),
        scratch_shapes=[
            VMEM((RANK, D_OUT), BF16),
            pltpu.SemaphoreType.DMA((2 + 2 * len(ROW_PARTS),)),
        ],
        compiler_params=pltpu.CompilerParams(vmem_limit_bytes=16 * 2**20),
        cost_estimate=pl.CostEstimate(
            flops=2 * 64 * TOKENS * D_IN, bytes_accessed=2 * TOKENS * D_IN * 2, transcendentals=0
        ),
        name="first_products",
    )(in_hbm(warm), in_hbm(grads), in_hbm(inputs), in_hbm(weight))
    return list(results) if ahead else [*results, None]


def gram_schmidt_steps(rows):
    place = lax.broadcasted_iota(jnp.int32, (RANK, 1), 0)
    lane = lax.broadcasted_iota(jnp.int32, (RANK, 128), 1)
    steps = (lax.broadcasted_iota(jnp.int32, (RANK, 128), 0) == lane).astype(F32)
    for rank in range(RANK):
        row = rows[rank : rank + 1]
        step = steps[rank : rank + 1]
        scale = lax.rsqrt(jnp.sum(row * row, axis=1, keepdims=True) + 1e-06)
        row = row * scale
        step = step * scale
        along = jnp.sum(rows * row, axis=1, keepdims=True)
        along = jnp.where(place > rank, along, 0.0)
        rows = rows - along * row
        steps = jnp.where(place == rank, step, steps - along * step)
    return steps


def applied(steps, value):
    result = steps[:, :1] * value[:1]
    for rank in range(1, RANK):
        result = result + steps[:, rank : rank + 1] * value[rank : rank + 1]
    return result


def second_kernel(*refs):
    *piece_refs, grads_ref, inputs_ref, left_ref, partial_ref = refs
    total = functools.reduce(lambda left, right: left + right, [ref[...] for ref in piece_refs])
    total = total * (1.0 / REPLICAS)
    left_ref[...] = total
    steps = gram_schmidt_steps(total)
    backward = folded(
        lax.dot_general(stacked(total), inputs_ref[...], NT, preferred_element_type=F32)
    )
    partial_value = folded(
        lax.dot_general(stacked(backward), grads_ref[...], NN, preferred_element_type=F32)
    )
    partial_ref[...] = (applied(steps, partial_value) * (1.0 / REPLICAS)).astype(
        partial_ref.dtype
    )


def second_products(pieces, grads, inputs):
    return pl.pallas_call(
        second_kernel,
        out_shape=(VMEM((RANK, D_IN), F32), VMEM((RANK, D_OUT), WIRE)),
        in_specs=[whole()] * (len(pieces) + 2),
        out_specs=(whole(), whole()),
        compiler_params=pltpu.CompilerParams(vmem_limit_bytes=16 * 2**20),
        cost_estimate=pl.CostEstimate(
            flops=2 * 64 * TOKENS * D_IN, bytes_accessed=RANK * D_IN * 24, transcendentals=0
        ),
        name="second_products",
    )(*[in_vmem(piece) for piece in pieces], in_vmem(grads), in_vmem(inputs))


def left_kernel(left_ref, out_hbm, sem):
    copy = pltpu.make_async_copy(left_ref, out_hbm, sem)
    copy.start()
    copy.wait()


def left_stored(left):
    return pl.pallas_call(
        left_kernel,
        out_shape=jax.ShapeDtypeStruct((RANK, D_IN), F32),
        in_specs=[whole()],
        out_specs=anywhere(),
        scratch_shapes=[pltpu.SemaphoreType.DMA],
        compiler_params=pltpu.CompilerParams(vmem_limit_bytes=2 * 2**20),
        name="left_stored",
    )(in_vmem(left))


def widened(*values):
    values = [value.astype(F32) for value in values]
    return functools.reduce(lambda left, right: left + right, values)


def product_kernel(base, sizes, ahead, grads_ref, *refs):
    held, streamed = sizes
    if held:
        held_ref, refs = refs[0], refs[1:]
    weight_hbm, out_ref, *refs = refs
    if ahead:
        ahead_ref, refs = refs[0], refs[1:]
    sems = refs[-1]
    streams = []
    for row in range(0, streamed, CHUNK):
        streams.append(
            pltpu.make_async_copy(
                weight_hbm.at[pl.ds(base + held + row, CHUNK)],
                refs[0].at[pl.ds(row, CHUNK)],
                sems.at[1 + row // CHUNK],
            )
        )
    for stream in streams:
        stream.start()
    if ahead:
        following = pltpu.make_async_copy(
            weight_hbm.at[pl.ds(base + held + streamed, ahead)], ahead_ref, sems.at[0]
        )
        following.start()

    def product(block_ref, row, column):
        out_ref[:, column : column + CHUNK] = lax.dot_general(
            grads_ref[...], block_ref[row : row + CHUNK, :], NT, preferred_element_type=F32
        ).astype(BF16)

    for row in range(0, held, CHUNK):
        product(held_ref, row, row)
    for row in range(0, streamed, CHUNK):
        streams[row // CHUNK].wait()
        product(refs[0], row, held + row)
    if ahead:
        following.wait()


def product_part(grads, held, weight, part):
    sizes = PARTS[part]
    ahead = PARTS[part + 1][0] if part + 1 < len(PARTS) else 0
    base = sum(sum(earlier) for earlier in PARTS[:part])
    operands = [in_vmem(grads)]
    if sizes[0]:
        operands.append(in_vmem(held))
    operands.append(in_hbm(weight))
    out_shape = [VMEM((TOKENS, sum(sizes)), BF16)]
    if ahead:
        out_shape.append(VMEM((ahead, D_OUT), BF16))
    scratch = [pltpu.SemaphoreType.DMA((1 + D_IN // CHUNK,))]
    if sizes[1]:
        scratch.insert(0, VMEM((sizes[1], D_OUT), BF16))
    return pl.pallas_call(
        functools.partial(product_kernel, base, sizes, ahead),
        out_shape=out_shape,
        in_specs=[whole()] * (len(operands) - 1) + [anywhere()],
        out_specs=[whole()] * len(out_shape),
        scratch_shapes=scratch,
        compiler_params=pltpu.CompilerParams(vmem_limit_bytes=32 * 2**20),
        cost_estimate=pl.CostEstimate(
            flops=2 * TOKENS * D_OUT * sum(sizes) // SHARE,
            bytes_accessed=sum(sizes) * D_OUT * 2 // SHARE,
            transcendentals=0,
        ),
        name="product_part",
    )(*operands)


def store_kernel(*refs):
    *pieces, out_hbm, zeros_ref, sems = refs

    def moved(sources):
        base = 0
        copies = []
        for place, source in enumerate(sources):
            width = source.shape[1]
            copies.append(
                pltpu.make_async_copy(source, out_hbm.at[:, pl.ds(base, width)], sems.at[place])
            )
            base += width
        for copy in copies:
            copy.start()
        for copy in copies:
            copy.wait()

    last = lax.axis_index("section") == SECTIONS - 1

    @pl.when(last)
    def _():
        zeros_ref[...] = jnp.zeros_like(zeros_ref)
        moved([zeros_ref] * (D_IN // CHUNK))

    @pl.when(jnp.logical_not(last))
    def _():
        moved(pieces)


def stored(pieces):
    return pl.pallas_call(
        store_kernel,
        out_shape=jax.ShapeDtypeStruct((TOKENS, D_IN), BF16),
        in_specs=[whole()] * len(pieces),
        out_specs=anywhere(),
        scratch_shapes=[
            VMEM((TOKENS, CHUNK), BF16),
            pltpu.SemaphoreType.DMA((D_IN // CHUNK,)),
        ],
        compiler_params=pltpu.CompilerParams(vmem_limit_bytes=8 * 2**20),
        cost_estimate=pl.CostEstimate(
            flops=0, bytes_accessed=4 * TOKENS * D_IN, transcendentals=0
        ),
        name="store",
    )(*[in_vmem(piece) for piece in pieces])


def replica(y, x, z):
    return (y % 4) * 8 + (x % 2) * 4 + z % 4


def moves(dy, dx, dz):
    return [
        (replica(y, x, z), replica(y + dy, x + dx, z + dz))
        for y in range(4)
        for x in range(2)
        for z in range(4)
    ]


def swaps(*masks):
    return [
        [
            (replica(y, x, z), replica(y ^ flip_y, x ^ flip_x, z ^ flip_z))
            for y in range(4)
            for x in range(2)
            for z in range(4)
        ]
        for flip_y, flip_x, flip_z in masks
    ]


X_ROUND = swaps((0, 1, 0))
Y_ROUND = swaps((1, 0, 0), (3, 0, 0), (2, 0, 0))
Z_ROUND = swaps((0, 0, 1), (0, 0, 3), (0, 0, 2))
LEFT_ROUNDS = [
    X_ROUND,
    swaps((0, 0, 3), (0, 0, 1), (0, 0, 2)),
    swaps((3, 0, 0), (1, 0, 0), (2, 0, 0)),
]
PART_OF_ROUND = {0: 0, 1: 1, 2: 2}
RIGHT_ROUNDS = [Z_ROUND, Y_ROUND, X_ROUND]


def sent(value, pattern):
    return [lax.ppermute(value, "dp", pairs) for pairs in pattern]


def tied(*values):
    return lax.optimization_barrier(values)


def handed(piece):
    return lax.ppermute(piece, "section", [(1, 0), (2, 1), (3, 2), (0, 3)])


def per_device(section_inputs, weights, output_grads, warm_start):
    weight = weights[0]
    value, grads, inputs, held = first_products(
        warm_start[0], output_grads[0], section_inputs[0], weight
    )

    arrived = []
    for place, pattern in enumerate(LEFT_ROUNDS):
        if place:
            value = widened(value, *arrivals)
            value, held = tied(value, held)
        arrivals = sent(value, pattern)
        part = PART_OF_ROUND.get(place)
        if part is not None:
            piece, *held = product_part(grads, held, weight, part)
            held = held[0] if held else piece
            arrived.append(handed(piece))
    *pieces, arrived[0], _ = tied(value, *arrivals, arrived[0], held)
    left, value = second_products(pieces, grads, inputs)

    for place, pattern in enumerate(RIGHT_ROUNDS):
        if place:
            value = widened(value, *arrivals).astype(WIRE)
        if place == len(RIGHT_ROUNDS) - 1:
            value, *arrived = tied(value, *arrived)
        elif place == 1:
            value, left_factor, *arrived[:-1] = tied(value, left_factor, *arrived[:-1])
        arrivals = sent(value, pattern)
        if not place:
            tied_left, _ = tied(left, value)
            left_factor = left_stored(tied_left)
    arrived = stored(arrived)
    right_factor = widened(value, *arrivals)
    return (arrived[None], left_factor[None], right_factor[None])


def solution(mesh):
    return jax.shard_map(
        per_device,
        mesh=mesh,
        in_specs=(
            P("section", "dp", None),
            P("section", None, None),
            P("section", "dp", None),
            P("section", None, None),
        ),
        out_specs=(P("section", "dp", None), P("section", None, None), P("section", None, None)),
        check_vma=False,
    )
```

```python
import functools

import jax
import jax.numpy as jnp
from jax import lax
from jax.experimental import pallas as pl
from jax.experimental.pallas import tpu as pltpu
from jax.sharding import PartitionSpec as P

TOKENS = 384
D_IN = 3072
D_OUT = 3072
RANK = 8
REPLICAS = 32
SECTIONS = 4
ROW_PARTS = (128, 128, 128)
WIRE = jnp.bfloat16
CHUNK = 512
SHARE = 4
PARTS = ((512, 512), (1024, 0), (1024, 0))

VMEM = pltpu.VMEM
F32 = jnp.float32
BF16 = jnp.bfloat16

NT = (((1,), (1,)), ((), ()))
NN = (((1,), (0,)), ((), ()))


def stacked(value):
    high = value.astype(BF16)
    rest = value - high.astype(F32)
    middle = rest.astype(BF16)
    low = (rest - middle.astype(F32)).astype(BF16)
    return jnp.concatenate([high, middle, low], axis=0)


def folded(value):
    return value[:RANK] + (value[RANK : 2 * RANK] + value[2 * RANK :])


def in_vmem(value):
    return pltpu.with_memory_space_constraint(value, VMEM)


def in_hbm(value):
    return pltpu.with_memory_space_constraint(value, pltpu.HBM)


def whole():
    return pl.BlockSpec(memory_space=VMEM)


def anywhere():
    return pl.BlockSpec(memory_space=pl.ANY)


def first_kernel(
    warm_hbm, grads_hbm, inputs_hbm, weight_hbm, partial_ref, grads_ref, inputs_ref, *refs
):
    ahead = PARTS[0][0]
    if ahead:
        ahead_ref, refs = refs[0], refs[1:]
    warm_ref, sems = refs
    warm_copy = pltpu.make_async_copy(warm_hbm, warm_ref, sems.at[0])
    warm_copy.start()
    spans = []
    copies = []
    first = 0
    for part, rows in enumerate(ROW_PARTS):
        span = pl.ds(first, rows)
        copies.append(
            (
                pltpu.make_async_copy(
                    grads_hbm.at[span], grads_ref.at[span], sems.at[2 + 2 * part]
                ),
                pltpu.make_async_copy(
                    inputs_hbm.at[span], inputs_ref.at[span], sems.at[3 + 2 * part]
                ),
            )
        )
        spans.append(slice(first, first + rows))
        first += rows
    for pair in copies:
        for copy in pair:
            copy.start()
    if ahead:
        ahead_copy = pltpu.make_async_copy(
            weight_hbm.at[pl.ds(0, ahead)], ahead_ref, sems.at[1]
        )
        ahead_copy.start()
    warm_copy.wait()
    total = None
    for span, (grads_copy, inputs_copy) in zip(spans, copies):
        grads_copy.wait()
        projected = stacked(
            lax.dot_general(warm_ref[...], grads_ref[span, :], NT, preferred_element_type=F32)
        )
        inputs_copy.wait()
        term = lax.dot_general(
            projected, inputs_ref[span, :], NN, preferred_element_type=F32
        )
        total = term if total is None else total + term
    partial_ref[...] = folded(total)
    if ahead:
        ahead_copy.wait()


def first_products(warm, grads, inputs, weight):
    ahead = PARTS[0][0]
    out_shape = [
        VMEM((RANK, D_IN), F32),
        VMEM((TOKENS, D_OUT), BF16),
        VMEM((TOKENS, D_IN), BF16),
    ]
    if ahead:
        out_shape.append(VMEM((ahead, D_OUT), BF16))
    results = pl.pallas_call(
        first_kernel,
        out_shape=out_shape,
        in_specs=[anywhere()] * 4,
        out_specs=[whole()] * len(out_shape),
        scratch_shapes=[
            VMEM((RANK, D_OUT), BF16),
            pltpu.SemaphoreType.DMA((2 + 2 * len(ROW_PARTS),)),
        ],
        compiler_params=pltpu.CompilerParams(vmem_limit_bytes=16 * 2**20),
        cost_estimate=pl.CostEstimate(
            flops=2 * 64 * TOKENS * D_IN, bytes_accessed=2 * TOKENS * D_IN * 2, transcendentals=0
        ),
        name="first_products",
    )(in_hbm(warm), in_hbm(grads), in_hbm(inputs), in_hbm(weight))
    return list(results) if ahead else [*results, None]


def gram_schmidt_steps(rows):
    place = lax.broadcasted_iota(jnp.int32, (RANK, 1), 0)
    lane = lax.broadcasted_iota(jnp.int32, (RANK, 128), 1)
    steps = (lax.broadcasted_iota(jnp.int32, (RANK, 128), 0) == lane).astype(F32)
    for rank in range(RANK):
        row = rows[rank : rank + 1]
        step = steps[rank : rank + 1]
        scale = lax.rsqrt(jnp.sum(row * row, axis=1, keepdims=True) + 1e-06)
        row = row * scale
        step = step * scale
        along = jnp.sum(rows * row, axis=1, keepdims=True)
        along = jnp.where(place > rank, along, 0.0)
        rows = rows - along * row
        steps = jnp.where(place == rank, step, steps - along * step)
    return steps


def applied(steps, value):
    result = steps[:, :1] * value[:1]
    for rank in range(1, RANK):
        result = result + steps[:, rank : rank + 1] * value[rank : rank + 1]
    return result


def second_kernel(*refs):
    *piece_refs, grads_ref, inputs_ref, left_ref, partial_ref = refs
    total = functools.reduce(lambda left, right: left + right, [ref[...] for ref in piece_refs])
    total = total * (1.0 / REPLICAS)
    left_ref[...] = total
    steps = gram_schmidt_steps(total)
    backward = folded(
        lax.dot_general(stacked(total), inputs_ref[...], NT, preferred_element_type=F32)
    )
    partial_value = folded(
        lax.dot_general(stacked(backward), grads_ref[...], NN, preferred_element_type=F32)
    )
    partial_ref[...] = (applied(steps, partial_value) * (1.0 / REPLICAS)).astype(
        partial_ref.dtype
    )


def second_products(pieces, grads, inputs):
    return pl.pallas_call(
        second_kernel,
        out_shape=(VMEM((RANK, D_IN), F32), VMEM((RANK, D_OUT), WIRE)),
        in_specs=[whole()] * (len(pieces) + 2),
        out_specs=(whole(), whole()),
        compiler_params=pltpu.CompilerParams(vmem_limit_bytes=16 * 2**20),
        cost_estimate=pl.CostEstimate(
            flops=2 * 64 * TOKENS * D_IN, bytes_accessed=RANK * D_IN * 24, transcendentals=0
        ),
        name="second_products",
    )(*[in_vmem(piece) for piece in pieces], in_vmem(grads), in_vmem(inputs))


def left_kernel(left_ref, out_hbm, sem):
    copy = pltpu.make_async_copy(left_ref, out_hbm, sem)
    copy.start()
    copy.wait()


def left_stored(left):
    return pl.pallas_call(
        left_kernel,
        out_shape=jax.ShapeDtypeStruct((RANK, D_IN), F32),
        in_specs=[whole()],
        out_specs=anywhere(),
        scratch_shapes=[pltpu.SemaphoreType.DMA],
        compiler_params=pltpu.CompilerParams(vmem_limit_bytes=2 * 2**20),
        name="left_stored",
    )(in_vmem(left))


def widened(*values):
    values = [value.astype(F32) for value in values]
    return functools.reduce(lambda left, right: left + right, values)


def product_kernel(base, sizes, ahead, grads_ref, *refs):
    held, streamed = sizes
    if held:
        held_ref, refs = refs[0], refs[1:]
    weight_hbm, out_ref, *refs = refs
    if ahead:
        ahead_ref, refs = refs[0], refs[1:]
    sems = refs[-1]
    streams = []
    for row in range(0, streamed, CHUNK):
        streams.append(
            pltpu.make_async_copy(
                weight_hbm.at[pl.ds(base + held + row, CHUNK)],
                refs[0].at[pl.ds(row, CHUNK)],
                sems.at[1 + row // CHUNK],
            )
        )
    for stream in streams:
        stream.start()
    if ahead:
        following = pltpu.make_async_copy(
            weight_hbm.at[pl.ds(base + held + streamed, ahead)], ahead_ref, sems.at[0]
        )
        following.start()

    def product(block_ref, row, column):
        out_ref[:, column : column + CHUNK] = lax.dot_general(
            grads_ref[...], block_ref[row : row + CHUNK, :], NT, preferred_element_type=F32
        ).astype(BF16)

    for row in range(0, held, CHUNK):
        product(held_ref, row, row)
    for row in range(0, streamed, CHUNK):
        streams[row // CHUNK].wait()
        product(refs[0], row, held + row)
    if ahead:
        following.wait()


def product_part(grads, held, weight, part):
    sizes = PARTS[part]
    ahead = PARTS[part + 1][0] if part + 1 < len(PARTS) else 0
    base = sum(sum(earlier) for earlier in PARTS[:part])
    operands = [in_vmem(grads)]
    if sizes[0]:
        operands.append(in_vmem(held))
    operands.append(in_hbm(weight))
    out_shape = [VMEM((TOKENS, sum(sizes)), BF16)]
    if ahead:
        out_shape.append(VMEM((ahead, D_OUT), BF16))
    scratch = [pltpu.SemaphoreType.DMA((1 + D_IN // CHUNK,))]
    if sizes[1]:
        scratch.insert(0, VMEM((sizes[1], D_OUT), BF16))
    return pl.pallas_call(
        functools.partial(product_kernel, base, sizes, ahead),
        out_shape=out_shape,
        in_specs=[whole()] * (len(operands) - 1) + [anywhere()],
        out_specs=[whole()] * len(out_shape),
        scratch_shapes=scratch,
        compiler_params=pltpu.CompilerParams(vmem_limit_bytes=32 * 2**20),
        cost_estimate=pl.CostEstimate(
            flops=2 * TOKENS * D_OUT * sum(sizes) // SHARE,
            bytes_accessed=sum(sizes) * D_OUT * 2 // SHARE,
            transcendentals=0,
        ),
        name="product_part",
    )(*operands)


def store_kernel(*refs):
    *pieces, out_hbm, zeros_ref, sems = refs

    def moved(sources):
        base = 0
        copies = []
        for place, source in enumerate(sources):
            width = source.shape[1]
            copies.append(
                pltpu.make_async_copy(source, out_hbm.at[:, pl.ds(base, width)], sems.at[place])
            )
            base += width
        for copy in copies:
            copy.start()
        for copy in copies:
            copy.wait()

    last = lax.axis_index("section") == SECTIONS - 1

    @pl.when(last)
    def _():
        zeros_ref[...] = jnp.zeros_like(zeros_ref)
        moved([zeros_ref] * (D_IN // CHUNK))

    @pl.when(jnp.logical_not(last))
    def _():
        moved(pieces)


def stored(pieces):
    return pl.pallas_call(
        store_kernel,
        out_shape=jax.ShapeDtypeStruct((TOKENS, D_IN), BF16),
        in_specs=[whole()] * len(pieces),
        out_specs=anywhere(),
        scratch_shapes=[
            VMEM((TOKENS, CHUNK), BF16),
            pltpu.SemaphoreType.DMA((D_IN // CHUNK,)),
        ],
        compiler_params=pltpu.CompilerParams(vmem_limit_bytes=8 * 2**20),
        cost_estimate=pl.CostEstimate(
            flops=0, bytes_accessed=4 * TOKENS * D_IN, transcendentals=0
        ),
        name="store",
    )(*[in_vmem(piece) for piece in pieces])


def replica(y, x, z):
    return (y % 4) * 8 + (x % 2) * 4 + z % 4


def moves(dy, dx, dz):
    return [
        (replica(y, x, z), replica(y + dy, x + dx, z + dz))
        for y in range(4)
        for x in range(2)
        for z in range(4)
    ]


def swaps(*masks):
    return [
        [
            (replica(y, x, z), replica(y ^ flip_y, x ^ flip_x, z ^ flip_z))
            for y in range(4)
            for x in range(2)
            for z in range(4)
        ]
        for flip_y, flip_x, flip_z in masks
    ]


X_ROUND = swaps((0, 1, 0))
Y_ROUND = swaps((1, 0, 0), (3, 0, 0), (2, 0, 0))
Z_ROUND = swaps((0, 0, 1), (0, 0, 3), (0, 0, 2))
LEFT_ROUNDS = [
    X_ROUND,
    swaps((0, 0, 3), (0, 0, 1), (0, 0, 2)),
    swaps((3, 0, 0), (1, 0, 0), (2, 0, 0)),
]
PART_OF_ROUND = {0: 0, 1: 1, 2: 2}
RIGHT_ROUNDS = [Z_ROUND, Y_ROUND, X_ROUND]


def sent(value, pattern):
    return [lax.ppermute(value, "dp", pairs) for pairs in pattern]


def tied(*values):
    return lax.optimization_barrier(values)


def handed(piece):
    return lax.ppermute(piece, "section", [(1, 0), (2, 1), (3, 2), (0, 3)])


def per_device(section_inputs, weights, output_grads, warm_start):
    weight = weights[0]
    value, grads, inputs, held = first_products(
        warm_start[0], output_grads[0], section_inputs[0], weight
    )

    arrived = []
    for place, pattern in enumerate(LEFT_ROUNDS):
        if place:
            value = widened(value, *arrivals)
            value, held = tied(value, held)
        arrivals = sent(value, pattern)
        part = PART_OF_ROUND.get(place)
        if part is not None:
            piece, *held = product_part(grads, held, weight, part)
            held = held[0] if held else piece
            arrived.append(handed(piece))
    *pieces, _ = tied(value, *arrivals, held)
    left, value = second_products(pieces, grads, inputs)

    for place, pattern in enumerate(RIGHT_ROUNDS):
        if place:
            value = widened(value, *arrivals).astype(WIRE)
        if place == len(RIGHT_ROUNDS) - 1:
            value, *arrived = tied(value, *arrived)
        elif place == 1:
            value, left_factor, *arrived[:-1] = tied(value, left_factor, *arrived[:-1])
        arrivals = sent(value, pattern)
        if not place:
            tied_left, _ = tied(left, value)
            left_factor = left_stored(tied_left)
    arrived = stored(arrived)
    right_factor = widened(value, *arrivals)
    return (arrived[None], left_factor[None], right_factor[None])


def solution(mesh):
    return jax.shard_map(
        per_device,
        mesh=mesh,
        in_specs=(
            P("section", "dp", None),
            P("section", None, None),
            P("section", "dp", None),
            P("section", None, None),
        ),
        out_specs=(P("section", "dp", None), P("section", None, None), P("section", None, None)),
        check_vma=False,
    )
```
